32 devices in a mesh: jobs: 2 (over y), gr: 4 (over x, core), gc: 4 (over z).
Axes of the slice: x: 2, y: 2, z: 4, core: 2. Of those that a mesh axis runs over, the one named last changes fastest.
Arguments:
- pair: bfloat16 [160, 80, 128], P(('jobs', 'gr'), 'gc'), parts along dimension 0, may hold values from -6 to 6
- mask: int32 [160], P('jobs'), parts along dimension 0, may hold values 0 or 1
- chain_ids: int32 [160], P('jobs'), parts along dimension 0, may hold values from 0 to 3, never falling along the last dimension, each value on 1 to 40 neighbouring positions
- attn_in: bfloat16 [2, 128, 512], replicated, may hold values from -0.5 to 0.5
- attn_out: bfloat16 [2, 128, 128], replicated, may hold values from -0.5 to 0.5
- bias_weight: bfloat16 [2, 128, 4], replicated, may hold values from -16 to 16
- chain_bias: float32 [2, 4], replicated, may hold values from -6 to 6
- trans_up: bfloat16 [128, 512], replicated, may hold values from -0.5 to 0.5
- trans_down: bfloat16 [512, 128], replicated, may hold values from -0.25 to 0.25
Outputs:
- result: bfloat16 [160, 80, 128], P(('jobs', 'gr'), 'gc'), parts along dimension 0
The draws below stay inside these ranges and needn't reach their ends.
There are 2 independent parts, one for each index of `jobs`. The reference program is written for one: setup_inputs(seed, part) draws one part's arguments, and reference() takes and returns one part's arrays. A program takes and returns all parts, laid end to end along the dimension named above; an argument that names none is the same for every part. Nothing has to cross between parts.
All inputs are finite; a program needn't handle non-finite values.
Results may differ from the reference program's by a relative error of at most 0.008.
The reference program's roundings to bfloat16 on the way count: a program that leaves them out, or rounds other values in their place, can miss the bound.
Values may be sent and summed in bfloat16 or wider, within the bound.
A program may use at most 64 MiB of HBM per device.

```python
import math
import jax
import jax.numpy as jnp
import numpy as np
from jax import lax

C = 128
HEADS = 4
FF = 512
TOKENS = 80
HEAD_DIM = 32


root_three = 1.7320508


def draw_bias_weight(key, part):
    base = jax.random.uniform(key, (2, C, HEADS), jnp.float32, -root_three, root_three)
    base = base / jnp.sqrt(jnp.float32(C))
    return base.astype(jnp.bfloat16)


def set_ends(entries, rng, low, largest):
    longest = entries.shape.index(max(entries.shape))
    spots = []
    for shift in (0, 1):
        where = [jax.random.randint(jax.random.fold_in(rng, axis), (), 0, length) for axis, length in enumerate(entries.shape)]
        where[longest] = (where[longest] + shift) % entries.shape[longest]
        spots.append(tuple(where))
    return entries.at[spots[0]].set(low).at[spots[1]].set(largest)


def steps_of(rng, shape, pieces, least, high):
    def one(axis_at, parts):
        steps = jax.random.uniform(jax.random.fold_in(jax.random.fold_in(rng, 6), axis_at), (parts,), jnp.float32, least / len(pieces), high / len(pieces))
        return jnp.repeat(jnp.exp(steps), shape[axis_at] // parts).reshape((-1,) + (1,) * (len(shape) - axis_at - 1))

    level = one(*pieces[0])
    for cut in pieces[1:]:
        level = level * one(*cut)
    return level


def length_profile(amount, total, bound, lean):
    weights = [(1 << 20) // math.isqrt(grade ** lean) + 1 for grade in range(2, amount + 1)]
    surplus, holding = total - bound - (amount - 1), [1] * (amount - 1)
    while surplus > 0:
        free = [i for i in range(amount - 1) if holding[i] < bound]
        whole, remaining = sum([weights[i] for i in free]), surplus
        for i in free:
            extra = min(bound - holding[i], max(1, remaining * weights[i] // whole), surplus)
            holding[i] = holding[i] + extra
            surplus = surplus - extra
    return np.array([bound] + holding)


def uneven(own_key, number_of, total, bound, lean):
    if number_of == 2:
        one = jax.random.randint(own_key, (), max(1, total - bound), min(bound, total - 1) + 1)
        return jnp.stack([one, total - one])
    tallies = jnp.asarray(length_profile(number_of, total, bound, lean), jnp.int32)
    pairs = (number_of - 1) // 2
    source_of, receiver = tallies[1:1 + 2 * pairs:2], tallies[2:2 + 2 * pairs:2]
    slack = jnp.minimum(source_of - 1, bound - receiver)
    moved = jax.random.randint(jax.random.fold_in(own_key, 1), (pairs,), 0, 1 << 20) % (slack + 1)
    tallies = tallies.at[1:1 + 2 * pairs:2].set(source_of - moved).at[2:2 + 2 * pairs:2].set(receiver + moved)
    return tallies[jax.random.permutation(jax.random.fold_in(own_key, 2), number_of)]


def centred(key, dims, deviation, reach, cuts=(), held_as=jnp.bfloat16):
    entries = jax.random.normal(key, dims, jnp.float32) * deviation
    if len(cuts) > 0:
        entries = steps_of(key, dims, cuts, -0.22, 0.18) * entries
    return jnp.clip(entries, min=-reach, max=reach).astype(held_as)


def setup_inputs(seed: int = 0, part: int = 0) -> dict:
    streams_of = jax.random.split(jax.random.key(seed), 10)
    part_keys = jax.random.split(jax.random.fold_in(streams_of[9], part), 10)
    return {
        "pair": centred(part_keys[0], (TOKENS, TOKENS, C), 1.0, 6.0, ((0, 4), (1, 4))),
        "mask": set_ends((jax.random.randint(part_keys[1], (TOKENS,), 0, 8) < 7).astype(jnp.int32), jax.random.fold_in(part_keys[1], 1), 0, 1),
        "chain_ids": jnp.searchsorted(jnp.cumsum(uneven(part_keys[2], 4, TOKENS, TOKENS // 2, 0)), jnp.arange(TOKENS), side="right").astype(jnp.int32),
        "attn_in": centred(streams_of[3], (2, C, 4 * C), C ** -0.5, 0.5),
        "attn_out": centred(streams_of[4], (2, C, C), C ** -0.5, 0.5),
        "bias_weight": draw_bias_weight(jax.random.fold_in(streams_of[9], 71), part),
        "chain_bias": centred(streams_of[6], (2, HEADS), 1.5, 6.0, (), jnp.float32),
        "trans_up": centred(streams_of[7], (C, FF), C ** -0.5, 0.5),
        "trans_down": centred(streams_of[8], (FF, C), FF ** -0.5, 0.25),
    }


def layer_norm(values):
    floats = values.astype(jnp.float32)
    center = lax.optimization_barrier(jnp.mean(floats, axis=-1, keepdims=True))
    spread = lax.optimization_barrier(jnp.mean((floats - center) ** 2, axis=-1, keepdims=True))
    return ((floats - center) * lax.rsqrt(spread + 1e-05)).astype(jnp.bfloat16)

def starting(pair, in_w, out_w, bias_w, chain_w, chain_ids, mask):
    normed = layer_norm(pair)
    flat = normed.reshape(-1, C)
    proj = jnp.dot(flat, in_w, preferred_element_type=jnp.float32).astype(jnp.bfloat16)
    proj = proj.reshape(TOKENS, TOKENS, 4 * C)
    same = (chain_ids[:, None] == chain_ids[None, :]).astype(jnp.float32)
    bias = jnp.dot(flat, bias_w, preferred_element_type=jnp.float32).reshape(TOKENS, TOKENS, HEADS)
    bias = bias + chain_w[None, None, :] * same[:, :, None]
    bias = jnp.transpose(bias, (2, 0, 1))
    maskadd = jnp.where(mask > 0, 0.0, -1000000000.0).astype(jnp.float32)
    scale = HEAD_DIM ** (-0.5)

    def one_row(piece):
        query = piece[:, 0:C].reshape(TOKENS, HEADS, HEAD_DIM).astype(jnp.float32)
        keys = piece[:, C:2 * C].reshape(TOKENS, HEADS, HEAD_DIM).astype(jnp.float32)
        vals = piece[:, 2 * C:3 * C].reshape(TOKENS, HEADS, HEAD_DIM).astype(jnp.float32)
        gate = piece[:, 3 * C:].astype(jnp.float32)
        scores = jnp.einsum('jhd,khd->hjk', query, keys) * scale + bias + maskadd[None, None, :]
        probs = jax.nn.softmax(scores, axis=-1).astype(jnp.bfloat16)
        mixed = jnp.einsum('hjk,khd->jhd', probs.astype(jnp.float32), vals).reshape(TOKENS, C)
        return (jax.nn.sigmoid(gate) * mixed).astype(jnp.bfloat16)
    gated = lax.map(one_row, proj)
    update = jnp.dot(gated.reshape(-1, C), out_w, preferred_element_type=jnp.float32).reshape(TOKENS, TOKENS, C)
    return (pair.astype(jnp.float32) + update).astype(jnp.bfloat16)

def reference(pair, mask, chain_ids, attn_in, attn_out, bias_weight, chain_bias, trans_up, trans_down):
    first = starting(pair, attn_in[0], attn_out[0], bias_weight[0], chain_bias[0], chain_ids, mask)
    normed = layer_norm(first).reshape(-1, C)
    hidden = jax.nn.relu(jnp.dot(normed, trans_up, preferred_element_type=jnp.float32)).astype(jnp.bfloat16)
    update = jnp.dot(hidden, trans_down, preferred_element_type=jnp.float32).reshape(TOKENS, TOKENS, C)
    second = (first.astype(jnp.float32) + update).astype(jnp.bfloat16)
    flipped = jnp.transpose(second, (1, 0, 2))
    ending = starting(flipped, attn_in[1], attn_out[1], bias_weight[1], chain_bias[1], chain_ids, mask)
    return jnp.transpose(ending, (1, 0, 2))
```

```python
import functools

import jax
import jax.numpy as jnp
from jax import lax
from jax.experimental import pallas as pl
from jax.experimental.pallas import tpu as pltpu
from jax.sharding import PartitionSpec as P

F32 = jnp.float32
BF16 = jnp.bfloat16
MESH = pl.DeviceIdType.MESH
LANES = 128
PADDED = -3e38


def padded_size(size):
    width = 16
    while width < size:
        width *= 2
    return width


def layer_norm(floats):
    center = jnp.mean(floats, axis=-1, keepdims=True)
    moved = floats - center
    spread = jnp.mean(moved * moved, axis=-1, keepdims=True)
    return (moved * lax.rsqrt(spread + 1e-05)).astype(BF16)


def dot(left, right):
    return jnp.dot(left, right, preferred_element_type=F32)


def dot_t(left, right):
    return lax.dot_general(left, right, (((1,), (1,)), ((), ())), preferred_element_type=F32)


class Phase:
    def __init__(self, count, width, n_p, n_s, p_axis, s_axis, chunks):
        self.P, self.S, self.Sp = count, width, padded_size(width)
        self.n_p, self.n_s, self.p_axis, self.s_axis = n_p, n_s, p_axis, s_axis
        self.unit = min(count, width)
        self.chunks = chunks
        self.rows = count // chunks
        self.keys = n_s * self.Sp
        group = max(1, 640 // self.keys)
        while self.rows % group:
            group -= 1
        self.group = group

    def scratch(self, heads, width):
        return [
            pltpu.VMEM((self.P, self.Sp, width), F32),
            pltpu.VMEM((self.n_s, self.P, self.Sp, width), BF16),
            pltpu.VMEM((self.P // self.unit, 8, self.unit * self.Sp), F32),
            pltpu.VMEM((self.S // self.unit, self.n_s, 8, self.unit * self.Sp), F32),
            pltpu.VMEM((heads, self.Sp, self.keys), F32),
            pltpu.SemaphoreType.DMA((self.chunks, self.n_s)),
            pltpu.SemaphoreType.DMA((self.chunks, self.n_s)),
            pltpu.SemaphoreType.DMA((self.P // self.unit, self.n_p)),
            pltpu.SemaphoreType.DMA((self.S // self.unit, self.n_s)),
        ]

    def device(self, p_index, s_index):
        return {self.p_axis: p_index, self.s_axis: s_index}

    def send_rows(self, refs, chunk):
        x, buf, _, _, _, send, recv, _, _ = refs
        mine = lax.axis_index(self.s_axis)
        rows = pl.ds(chunk * self.rows, self.rows)
        buf[mine, rows] = layer_norm(x[rows])
        for step in range(1, self.n_s):
            peer = lax.rem(mine + step, self.n_s)
            pltpu.make_async_remote_copy(
                src_ref=buf.at[mine, rows],
                dst_ref=buf.at[mine, rows],
                send_sem=send.at[chunk, step],
                recv_sem=recv.at[chunk, mine],
                device_id=self.device(lax.axis_index(self.p_axis), peer),
                device_id_type=MESH,
            ).start()

    def wait_rows(self, refs, chunk):
        _, buf, _, _, _, _, recv, _, _ = refs
        mine = lax.axis_index(self.s_axis)
        rows = pl.ds(chunk * self.rows, self.rows)
        for step in range(1, self.n_s):
            peer = lax.rem(mine + step, self.n_s)
            spot = buf.at[peer, rows]
            pltpu.make_async_copy(spot, spot, recv.at[chunk, peer]).wait()

    def piece(self, k):
        start = lax.axis_index(self.p_axis) * self.P + k * self.unit
        return start // self.S, lax.rem(start, self.S) // self.unit

    def bias_copies(self, refs, begin):
        _, _, part, got, _, _, _, send, recv = refs
        mine_p, mine_s = lax.axis_index(self.p_axis), lax.axis_index(self.s_axis)
        for k in range(self.P // self.unit):
            target, slot = self.piece(k)
            for step in range(self.n_p):
                row = lax.rem(mine_p + step, self.n_p)
                copy = pltpu.make_async_remote_copy(
                    src_ref=part.at[k],
                    dst_ref=got.at[slot, mine_s],
                    send_sem=send.at[k, step],
                    recv_sem=recv.at[slot, mine_s],
                    device_id=self.device(row, target),
                    device_id_type=MESH,
                )
                act = copy.start if begin else copy.wait_send
                if step > 0:
                    act()
                    continue
                pl.when(target != mine_s)(act)
                if begin:

                    @pl.when(target == mine_s)
                    def _():
                        pltpu.make_async_copy(
                            part.at[k], got.at[slot, mine_s], recv.at[slot, mine_s]
                        ).start()

    def send_bias(self, refs, weight):
        _, buf, part, _, _, _, _, _, _ = refs
        mine = lax.axis_index(self.s_axis)
        for k in range(self.P // self.unit):
            own = buf[mine, k * self.unit : (k + 1) * self.unit]
            part[k] = dot_t(weight, own.reshape(self.unit * self.Sp, own.shape[-1]))[:8]
        self.bias_copies(refs, True)

    def finish_bias(self, refs, extra):
        _, _, _, got, bias, _, _, _, recv = refs
        bias[...] = extra[...]
        heads = bias.shape[0]
        share = max(1, LANES // self.Sp)
        for ks in range(self.S // self.unit):
            for b in range(self.n_s):
                spot = got.at[ks, b]
                pltpu.make_async_copy(spot, spot, recv.at[ks, b]).wait()
        lane = lax.broadcasted_iota(jnp.int32, (8, LANES), 1) // min(self.Sp, LANES)
        for ks in range(self.S // self.unit):
            for q in range(self.unit):
                tile, off = (q * self.Sp) // LANES, (q * self.Sp) % LANES
                for first in range(0, self.n_s, share):
                    total = None
                    for b in range(first, min(first + share, self.n_s)):
                        turn = ((b - first) * self.Sp - off) % LANES
                        value = got[ks, b, :, tile * LANES : (tile + 1) * LANES]
                        if turn:
                            value = pltpu.roll(value, turn, 1)
                        total = value if total is None else jnp.where(lane == b - first, value, total)
                    where = first * self.Sp
                    width = min(LANES, self.keys - where)
                    spot = ks * self.unit + q
                    for h in range(heads):
                        bias[h, spot : spot + 1, where : where + width] += total[h : h + 1, :width]

    def wait_sends(self, refs):
        _, buf, _, _, _, send, _, _, _ = refs
        mine = lax.axis_index(self.s_axis)
        for chunk in range(self.chunks):
            rows = pl.ds(chunk * self.rows, self.rows)
            spot = buf.at[mine, rows]
            for step in range(1, self.n_s):
                pltpu.make_async_copy(spot, spot, send.at[chunk, step]).wait()
        self.bias_copies(refs, False)

    def attend(self, refs, in_w, out_w, maskrow, consume):
        x, buf, _, _, bias, _, _, _, _ = refs
        heads, width = bias.shape[0], x.shape[-1]
        head_width = width // heads
        scale = head_width ** (-0.5)
        mine = lax.axis_index(self.s_axis)
        Sp, group = self.Sp, self.group
        which = lax.broadcasted_iota(jnp.int32, (heads, 1, width), 2) // head_width
        select = which == lax.broadcasted_iota(jnp.int32, (heads, 1, width), 0)
        select_f = select.astype(F32)

        def step(start):
            rows = pl.ds(start, group)
            normed = buf[:, rows].reshape(self.n_s * group * Sp, width)
            own = buf[mine, rows].reshape(group * Sp, width)
            keys = dot(normed, in_w[:, width : 2 * width]).astype(BF16)
            vals = dot(normed, in_w[:, 2 * width : 3 * width]).astype(BF16)
            keys = keys.reshape(self.n_s, group, Sp, width)
            vals = vals.reshape(self.n_s, group, Sp, width)
            query = dot(own, in_w[:, :width]).astype(BF16).astype(F32).reshape(group, Sp, width)
            gate = dot(own, in_w[:, 3 * width :]).astype(BF16).astype(F32)
            table = bias[...].reshape(heads * Sp, self.keys)
            hidden = maskrow[...]
            mixed = []
            for r in range(group):
                split = (query[r][None] * select_f).astype(BF16).reshape(heads * Sp, width)
                scores = dot_t(split, keys[:, r].reshape(self.keys, width)) * scale
                scores = (scores + table) + hidden
                top = jnp.max(scores, axis=-1, keepdims=True)
                weights = jnp.exp(scores - top)
                norm = jnp.sum(weights, axis=-1, keepdims=True)
                probs = (weights * (1.0 / norm)).astype(BF16)
                out = dot(probs, vals[:, r].reshape(self.keys, width)).reshape(heads, Sp, width)
                mixed.append(jnp.sum(jnp.where(select, out, 0.0), axis=0))
            mixed = mixed[0] if group == 1 else jnp.concatenate(mixed, axis=0)
            gated = (jax.nn.sigmoid(gate) * mixed).astype(BF16)
            old = x[rows].reshape(group * Sp, width)
            consume(start, (old + dot(gated, out_w[...])).astype(BF16).astype(F32))

        @pl.loop(0, self.chunks)
        def _(chunk):
            self.wait_rows(refs, chunk)

            @pl.loop(0, self.rows // group)
            def _(index):
                step(chunk * self.rows + index * group)


def kernel(phases, sizes, pair, extra0, extra1, mask0, mask1, in_w, out_w, bias_w, up, down, result, *scratch):
    n_gr, n_gc = sizes
    one, two = phases
    refs1, refs2 = scratch[:9], scratch[9:18]
    middle, ending = scratch[18:]
    x1, x2 = refs1[0], refs2[0]
    gr, gc = lax.axis_index("gr"), lax.axis_index("gc")
    barrier = pltpu.get_barrier_semaphore()
    for dr in range(n_gr):
        for dc in range(n_gc):
            if dr or dc:
                peer = {"gr": lax.rem(gr + dr, n_gr), "gc": lax.rem(gc + dc, n_gc)}
                pl.semaphore_signal(barrier, inc=1, device_id=peer, device_id_type=MESH)
    x1[...] = jnp.zeros_like(x1)
    x2[...] = jnp.zeros_like(x2)
    x1[:, : one.S, :] = pair[...].astype(F32)
    pl.semaphore_wait(barrier, n_gr * n_gc - 1)
    for chunk in range(one.chunks):
        one.send_rows(refs1, chunk)
    one.send_bias(refs1, bias_w[0])
    one.finish_bias(refs1, extra0)

    def transition(start, first):
        hidden = jnp.maximum(dot(layer_norm(first), up[...]), 0.0).astype(BF16)
        second = (first + dot(hidden, down[...])).astype(BF16).astype(F32)
        middle[pl.ds(pl.multiple_of(start * one.Sp, 8), one.group * one.Sp), :] = second

    one.attend(refs1, in_w.at[0], out_w.at[0], mask0, transition)
    for column in range(two.P):
        x2[column, : two.S, :] = middle[pl.ds(column, two.S, stride=one.Sp), :]
    for chunk in range(two.chunks):
        two.send_rows(refs2, chunk)
    two.send_bias(refs2, bias_w[1])
    two.finish_bias(refs2, extra1)

    def keep(start, final):
        ending[pl.ds(pl.multiple_of(start * two.Sp, 8), two.group * two.Sp), :] = final

    two.attend(refs2, in_w.at[1], out_w.at[1], mask1, keep)
    for row in range(one.P):
        result[row] = ending[pl.ds(row, one.S, stride=two.Sp), :].astype(BF16)
    one.wait_sends(refs1)
    two.wait_sends(refs2)


def key_row(values, phase, fill):
    values = values.reshape(phase.n_s, phase.S)
    values = jnp.pad(values, ((0, 0), (0, phase.Sp - phase.S)), constant_values=fill)
    return values.reshape(1, phase.keys)


def chain_term(chain_ids, weights, phase):
    own = lax.dynamic_slice_in_dim(chain_ids, lax.axis_index(phase.s_axis) * phase.S, phase.S)
    own = jnp.pad(own, (0, phase.Sp - phase.S), constant_values=-1)
    same = (own[:, None] == key_row(chain_ids, phase, -2)).astype(F32)
    return weights[:, None, None] * same[None]


def per_device(phases, sizes, pair, mask, chain_ids, attn_in, attn_out, bias_weight, chain_bias, trans_up, trans_down):
    one, two = phases
    width, heads = bias_weight.shape[1:]
    maskadd = jnp.where(mask > 0, 0.0, -1000000000.0).astype(F32)
    extras = [chain_term(chain_ids, chain_bias[a], phase) for a, phase in enumerate(phases)]
    masks = [key_row(maskadd, phase, PADDED) for phase in phases]
    bias_t = jnp.pad(jnp.transpose(bias_weight, (0, 2, 1)), ((0, 0), (0, 16 - heads), (0, 0)))
    vmem = pl.BlockSpec(memory_space=pltpu.VMEM)
    return pl.pallas_call(
        functools.partial(kernel, phases, sizes),
        out_shape=jax.ShapeDtypeStruct(pair.shape, BF16),
        in_specs=[vmem] * 10,
        out_specs=vmem,
        scratch_shapes=[
            *one.scratch(heads, width),
            *two.scratch(heads, width),
            pltpu.VMEM((one.P * one.Sp, width), F32),
            pltpu.VMEM((two.P * two.Sp, width), F32),
        ],
        compiler_params=pltpu.CompilerParams(
            collective_id=0, has_side_effects=True, vmem_limit_bytes=60 * 2**20
        ),
    )(pair, *extras, *masks, attn_in, attn_out, bias_t, trans_up, trans_down)


def solution(mesh):
    sizes = (mesh.shape["gr"], mesh.shape["gc"])
    jobs = mesh.shape["jobs"]

    def whole(pair, *others):
        rows, columns = pair.shape[0] // (jobs * sizes[0]), pair.shape[1] // sizes[1]
        chunks = 4
        while rows % chunks or columns % chunks:
            chunks -= 1
        phases = (
            Phase(rows, columns, sizes[0], sizes[1], "gr", "gc", chunks),
            Phase(columns, rows, sizes[1], sizes[0], "gc", "gr", chunks),
        )
        in_specs = (P(("jobs", "gr"), "gc", None), P("jobs"), P("jobs"), P(), P(), P(), P(), P(), P())
        return jax.shard_map(
            functools.partial(per_device, phases, sizes),
            mesh=mesh,
            in_specs=in_specs,
            out_specs=P(("jobs", "gr"), "gc", None),
            check_vma=False,
        )(pair, *others)

    return whole
```

```python
import functools

import jax
import jax.numpy as jnp
from jax import lax
from jax.experimental import pallas as pl
from jax.experimental.pallas import tpu as pltpu
from jax.sharding import PartitionSpec as P

F32 = jnp.float32
BF16 = jnp.bfloat16
MESH = pl.DeviceIdType.MESH
LANES = 128
PADDED = -3e38


def padded_size(size):
    width = 16
    while width < size:
        width *= 2
    return width


def layer_norm(floats):
    center = jnp.mean(floats, axis=-1, keepdims=True)
    moved = floats - center
    spread = jnp.mean(moved * moved, axis=-1, keepdims=True)
    return (moved * lax.rsqrt(spread + 1e-05)).astype(BF16)


def dot(left, right):
    return jnp.dot(left, right, preferred_element_type=F32)


def dot_t(left, right):
    return lax.dot_general(left, right, (((1,), (1,)), ((), ())), preferred_element_type=F32)


class Phase:
    def __init__(self, count, width, n_p, n_s, p_axis, s_axis, chunks):
        self.P, self.S, self.Sp = count, width, padded_size(width)
        self.n_p, self.n_s, self.p_axis, self.s_axis = n_p, n_s, p_axis, s_axis
        self.unit = min(count, width)
        self.chunks = chunks
        self.rows = count // chunks
        self.keys = n_s * self.Sp
        group = max(1, 640 // self.keys)
        while self.rows % group:
            group -= 1
        self.group = group

    def scratch(self, heads, width):
        return [
            pltpu.VMEM((self.P * self.S + self.Sp, width), F32),
            pltpu.VMEM((self.n_s, self.P * self.S, width), BF16),
            pltpu.VMEM((self.P // self.unit, heads, self.unit * self.Sp), F32),
            pltpu.VMEM((self.S // self.unit, self.n_s, heads, self.unit * self.Sp), F32),
            pltpu.VMEM((heads, self.Sp, self.keys), F32),
            pltpu.SemaphoreType.DMA((self.chunks, self.n_s)),
            pltpu.SemaphoreType.DMA((self.chunks, self.n_s)),
            pltpu.SemaphoreType.DMA((self.P // self.unit, self.n_p)),
            pltpu.SemaphoreType.DMA((self.S // self.unit, self.n_s)),
            pltpu.VMEM((self.n_s, self.rows * self.S + self.Sp, width), F32),
            pltpu.VMEM((self.P * self.S + self.Sp, width), F32),
            pltpu.VMEM((8, self.keys), F32),
        ]

    def span(self, chunk):
        size = self.rows * self.S
        return pl.ds(pl.multiple_of(chunk * size, 16), size)

    def norm_rows(self, refs, chunk):
        x, buf = refs[:2]
        own = refs[10]
        rows = self.span(chunk)
        normed = layer_norm(x[rows])
        own[rows] = normed.astype(F32)
        buf[lax.axis_index(self.s_axis), rows] = normed

    def padded(self, tokens):
        row = lax.broadcasted_iota(jnp.int32, tokens.shape, 0)
        return jnp.where(row < self.S, tokens, 0.0).astype(BF16)

    def key_row(self, refs, values, fill):
        base = refs[11]
        base[...] = jnp.zeros_like(base)
        base[:, : self.n_s * self.S] = jnp.broadcast_to(values.astype(F32), (8, self.n_s * self.S))
        plain = base[...]
        lane = lax.broadcasted_iota(jnp.int32, plain.shape, 1)
        row = plain
        for b in range(1, self.n_s):
            turned = pltpu.roll(plain, (b * (self.Sp - self.S)) % self.keys, 1)
            row = jnp.where(lane // self.Sp == b, turned, row)
        return plain, jnp.where(lane % self.Sp < self.S, row, fill)

    def chain_row(self, refs, bias, weights, chain_ids):
        plain, row = self.key_row(refs, chain_ids, -2.0)
        shape = (self.Sp, self.keys)
        lane = lax.broadcasted_iota(jnp.int32, shape, 1)
        spot = lax.broadcasted_iota(jnp.int32, shape, 0) + lax.axis_index(self.s_axis) * self.S
        own = jnp.sum(jnp.where(lane == spot, plain[:1], 0.0), axis=-1, keepdims=True)
        same = jnp.where(own == row[:1], 1.0, 0.0)
        for h in range(bias.shape[0]):
            bias[h] = weights(h) * same

    def device(self, p_index, s_index):
        return {self.p_axis: p_index, self.s_axis: s_index}

    def send_rows(self, refs, chunk):
        x, buf, _, _, _, send, recv = refs[:7]
        mine = lax.axis_index(self.s_axis)
        rows = self.span(chunk)
        for step in range(1, self.n_s):
            peer = lax.rem(mine + step, self.n_s)
            pltpu.make_async_remote_copy(
                src_ref=buf.at[mine, rows],
                dst_ref=buf.at[mine, rows],
                send_sem=send.at[chunk, step],
                recv_sem=recv.at[chunk, mine],
                device_id=self.device(lax.axis_index(self.p_axis), peer),
                device_id_type=MESH,
            ).start()

    def wait_rows(self, refs, chunk):
        _, buf, _, _, _, _, recv = refs[:7]
        mine = lax.axis_index(self.s_axis)
        rows = self.span(chunk)
        for step in range(1, self.n_s):
            peer = lax.rem(mine + step, self.n_s)
            spot = buf.at[peer, rows]
            pltpu.make_async_copy(spot, spot, recv.at[chunk, peer]).wait()

    def piece(self, k):
        start = lax.axis_index(self.p_axis) * self.P + k * self.unit
        return start // self.S, lax.rem(start, self.S) // self.unit

    def bias_copies(self, refs, begin):
        _, _, part, got, _, _, _, send, recv = refs[:9]
        mine_p, mine_s = lax.axis_index(self.p_axis), lax.axis_index(self.s_axis)
        for k in range(self.P // self.unit):
            target, slot = self.piece(k)
            for step in range(self.n_p):
                row = lax.rem(mine_p + step, self.n_p)
                copy = pltpu.make_async_remote_copy(
                    src_ref=part.at[k],
                    dst_ref=got.at[slot, mine_s],
                    send_sem=send.at[k, step],
                    recv_sem=recv.at[slot, mine_s],
                    device_id=self.device(row, target),
                    device_id_type=MESH,
                )
                act = copy.start if begin else copy.wait_send
                if step > 0:
                    act()
                    continue
                pl.when(target != mine_s)(act)
                if begin:

                    @pl.when(target == mine_s)
                    def _():
                        pltpu.make_async_copy(
                            part.at[k], got.at[slot, mine_s], recv.at[slot, mine_s]
                        ).start()

    def send_bias(self, refs, weight):
        part, tokens = refs[2], refs[10]
        for k in range(self.P // self.unit):
            starts = [(k * self.unit + q) * self.S for q in range(self.unit)]
            own = [self.padded(tokens[at : at + self.Sp]) for at in starts]
            part[k] = dot_t(weight, jnp.concatenate(own, axis=0))
        self.bias_copies(refs, True)

    def finish_bias(self, refs):
        _, _, _, got, bias, _, _, _, recv = refs[:9]
        heads = bias.shape[0]
        share = max(1, LANES // self.Sp)
        for ks in range(self.S // self.unit):
            for b in range(self.n_s):
                spot = got.at[ks, b]
                pltpu.make_async_copy(spot, spot, recv.at[ks, b]).wait()
        lane = lax.broadcasted_iota(jnp.int32, (heads, LANES), 1) // min(self.Sp, LANES)
        for ks in range(self.S // self.unit):
            for q in range(self.unit):
                tile, off = (q * self.Sp) // LANES, (q * self.Sp) % LANES
                for first in range(0, self.n_s, share):
                    total = None
                    for b in range(first, min(first + share, self.n_s)):
                        turn = ((b - first) * self.Sp - off) % LANES
                        value = got[ks, b, :, tile * LANES : (tile + 1) * LANES]
                        if turn:
                            value = pltpu.roll(value, turn, 1)
                        total = value if total is None else jnp.where(lane == b - first, value, total)
                    where = first * self.Sp
                    width = min(LANES, self.keys - where)
                    spot = ks * self.unit + q
                    for h in range(heads):
                        bias[h, spot : spot + 1, where : where + width] += total[h : h + 1, :width]

    def wait_sends(self, refs):
        _, buf, _, _, _, send = refs[:6]
        mine = lax.axis_index(self.s_axis)
        for chunk in range(self.chunks):
            rows = self.span(chunk)
            spot = buf.at[mine, rows]
            for step in range(1, self.n_s):
                pltpu.make_async_copy(spot, spot, send.at[chunk, step]).wait()
        self.bias_copies(refs, False)

    def attend(self, refs, in_w, out_w, maskrow, consume):
        x, buf, _, _, bias = refs[:5]
        stage = refs[9]
        heads, width = bias.shape[0], x.shape[-1]
        head_width = width // heads
        scale = head_width ** (-0.5)
        mine = lax.axis_index(self.s_axis)
        Sp, group = self.Sp, self.group
        which = lax.broadcasted_iota(jnp.int32, (heads, 1, width), 2) // head_width
        select = which == lax.broadcasted_iota(jnp.int32, (heads, 1, width), 0)
        select_f = select.astype(F32)

        def step(chunk, index):
            local = index * (group * self.S)
            places = [local + r * self.S for r in range(group)]
            normed = [
                self.padded(stage[b, pl.ds(at, Sp)]) for at in places for b in range(self.n_s)
            ]
            normed = jnp.concatenate(normed, axis=0)
            own = jnp.concatenate([self.padded(stage[mine, pl.ds(at, Sp)]) for at in places], axis=0)
            keys = dot(normed, in_w[:, width : 2 * width]).astype(BF16)
            vals = dot(normed, in_w[:, 2 * width : 3 * width]).astype(BF16)
            keys = keys.reshape(group, self.keys, width)
            vals = vals.reshape(group, self.keys, width)
            query = dot(own, in_w[:, :width]).astype(BF16).astype(F32).reshape(group, Sp, width)
            gate = dot(own, in_w[:, 3 * width :]).astype(BF16).astype(F32)
            table = bias[...].reshape(heads * Sp, self.keys)
            hidden = maskrow[:1]
            mixed = []
            for r in range(group):
                split = (query[r][None] * select_f).astype(BF16).reshape(heads * Sp, width)
                scores = dot_t(split, keys[r]) * scale
                scores = (scores + table) + hidden
                top = jnp.max(scores, axis=-1, keepdims=True)
                weights = jnp.exp(scores - top)
                norm = jnp.sum(weights, axis=-1, keepdims=True)
                probs = (weights * (1.0 / norm)).astype(BF16)
                out = dot(probs, vals[r]).reshape(heads, Sp, width)
                mixed.append(jnp.sum(jnp.where(select, out, 0.0), axis=0))
            mixed = mixed[0] if group == 1 else jnp.concatenate(mixed, axis=0)
            gated = (jax.nn.sigmoid(gate) * mixed).astype(BF16)
            begin = chunk * (self.rows * self.S)
            old = jnp.concatenate([x[pl.ds(begin + at, Sp)] for at in places], axis=0)
            consume(chunk * self.rows + index * group, (old + dot(gated, out_w[...])).astype(BF16).astype(F32))

        @pl.loop(0, self.chunks)
        def _(chunk):
            self.wait_rows(refs, chunk)
            for b in range(self.n_s):
                stage[b, : self.rows * self.S] = buf[b, self.span(chunk)].astype(F32)
            if self.rows == group:
                step(chunk, 0)
            else:
                pl.loop(0, self.rows // group)(lambda index: step(chunk, index))


def send_all(phase, refs, weight):
    phase.norm_rows(refs, 0)
    phase.send_rows(refs, 0)
    for chunk in range(1, phase.chunks):
        phase.norm_rows(refs, chunk)
    phase.send_bias(refs, weight)
    for chunk in range(1, phase.chunks):
        phase.send_rows(refs, chunk)


def kernel(phases, sizes, pair, mask, chain_ids, chain_w, in_w, out_w, bias_w, up, down, result, *scratch):
    n_gr, n_gc = sizes
    one, two = phases
    refs1, refs2 = scratch[:12], scratch[12:24]
    middle, ending, mask1, mask2 = scratch[24:]
    x1, x2 = refs1[0], refs2[0]
    gr, gc = lax.axis_index("gr"), lax.axis_index("gc")
    barrier = pltpu.get_barrier_semaphore()
    for dr in range(n_gr):
        for dc in range(n_gc):
            if dr or dc:
                peer = {"gr": lax.rem(gr + dr, n_gr), "gc": lax.rem(gc + dc, n_gc)}
                pl.semaphore_signal(barrier, inc=1, device_id=peer, device_id_type=MESH)
    for phase, refs in ((one, refs1), (two, refs2)):
        for ref, used in ((refs[0], phase.P * phase.S), (refs[10], phase.P * phase.S)):
            ref[used:] = jnp.zeros((phase.Sp, ref.shape[-1]), F32)
        for b in range(phase.n_s):
            refs[9][b, phase.rows * phase.S :] = jnp.zeros((phase.Sp, x1.shape[-1]), F32)
    for row in range(one.P):
        x1[row * one.S : (row + 1) * one.S] = pair[row].astype(F32)
    maskadd = jnp.where(mask[...] > 0, 0.0, -1000000000.0).astype(F32)
    for a, phase, refs, hidden in ((0, one, refs1, mask1), (1, two, refs2, mask2)):
        phase.chain_row(refs, refs[4], lambda h, a=a: chain_w[a, h], chain_ids[...])
        hidden[...] = phase.key_row(refs, maskadd, PADDED)[1]
    pl.semaphore_wait(barrier, n_gr * n_gc - 1)
    send_all(one, refs1, bias_w[0])
    one.finish_bias(refs1)

    def transition(start, first):
        hidden = jnp.maximum(dot(layer_norm(first), up[...]), 0.0).astype(BF16)
        second = (first + dot(hidden, down[...])).astype(BF16).astype(F32)
        middle[pl.ds(pl.multiple_of(start * one.Sp, 8), one.group * one.Sp), :] = second

    one.attend(refs1, in_w.at[0], out_w.at[0], mask1, transition)
    for column in range(two.P):
        x2[column * two.S : (column + 1) * two.S] = middle[pl.ds(column, two.S, stride=one.Sp), :]
    send_all(two, refs2, bias_w[1])
    two.finish_bias(refs2)

    def keep(start, final):
        ending[pl.ds(pl.multiple_of(start * two.Sp, 8), two.group * two.Sp), :] = final

    two.attend(refs2, in_w.at[1], out_w.at[1], mask2, keep)
    for row in range(one.P):
        result[row] = ending[pl.ds(row, one.S, stride=two.Sp), :].astype(BF16)
    one.wait_sends(refs1)
    two.wait_sends(refs2)


def per_device(phases, sizes, pair, mask, chain_ids, attn_in, attn_out, bias_weight, chain_bias, trans_up, trans_down):
    one, two = phases
    width, heads = bias_weight.shape[1:]
    vmem = pl.BlockSpec(memory_space=pltpu.VMEM)
    smem = pl.BlockSpec(memory_space=pltpu.SMEM)
    return pl.pallas_call(
        functools.partial(kernel, phases, sizes),
        out_shape=jax.ShapeDtypeStruct(pair.shape, BF16),
        in_specs=[vmem] * 3 + [smem] + [vmem] * 5,
        out_specs=vmem,
        scratch_shapes=[
            *one.scratch(heads, width),
            *two.scratch(heads, width),
            pltpu.VMEM((one.P * one.Sp, width), F32),
            pltpu.VMEM((two.P * two.Sp, width), F32),
            pltpu.VMEM((8, one.keys), F32),
            pltpu.VMEM((8, two.keys), F32),
        ],
        compiler_params=pltpu.CompilerParams(
            collective_id=0, has_side_effects=True, vmem_limit_bytes=60 * 2**20
        ),
    )(
        pair,
        mask.reshape(1, -1),
        chain_ids.reshape(1, -1),
        chain_bias,
        attn_in,
        attn_out,
        jnp.transpose(bias_weight, (0, 2, 1)),
        trans_up,
        trans_down,
    )


def solution(mesh):
    sizes = (mesh.shape["gr"], mesh.shape["gc"])
    jobs = mesh.shape["jobs"]

    def whole(pair, *others):
        rows, columns = pair.shape[0] // (jobs * sizes[0]), pair.shape[1] // sizes[1]
        chunks = 5
        while rows % chunks or columns % chunks or (rows * columns // chunks) % 16:
            chunks -= 1
        phases = (
            Phase(rows, columns, sizes[0], sizes[1], "gr", "gc", chunks),
            Phase(columns, rows, sizes[1], sizes[0], "gc", "gr", chunks),
        )
        in_specs = (P(("jobs", "gr"), "gc", None), P("jobs"), P("jobs"), P(), P(), P(), P(), P(), P())
        return jax.shard_map(
            functools.partial(per_device, phases, sizes),
            mesh=mesh,
            in_specs=in_specs,
            out_specs=P(("jobs", "gr"), "gc", None),
            check_vma=False,
        )(pair, *others)

    return whole
```

```python
import functools

import jax
import jax.numpy as jnp
from jax import lax
from jax.experimental import pallas as pl
from jax.experimental.pallas import tpu as pltpu
from jax.sharding import PartitionSpec as P

F32 = jnp.float32
BF16 = jnp.bfloat16
MESH = pl.DeviceIdType.MESH
LANES = 128
PADDED = -3e38
BATCHES = ((0, 1), (2, 3, 4))


def padded_size(size):
    width = 16
    while width < size:
        width *= 2
    return width


def aligned(start):
    return start if isinstance(start, int) else pl.multiple_of(start, 16)


def layer_norm(floats):
    center = jnp.mean(floats, axis=-1, keepdims=True)
    moved = floats - center
    spread = jnp.mean(moved * moved, axis=-1, keepdims=True)
    return (moved * lax.rsqrt(spread + 1e-05)).astype(BF16)


def dot(left, right):
    return jnp.dot(left, right, preferred_element_type=F32)


def dot_t(left, right):
    return lax.dot_general(left, right, (((1,), (1,)), ((), ())), preferred_element_type=F32)


class Phase:
    def __init__(self, count, width, n_p, n_s, p_axis, s_axis, chunks):
        self.P, self.S, self.Sp = count, width, padded_size(width)
        self.n_p, self.n_s, self.p_axis, self.s_axis = n_p, n_s, p_axis, s_axis
        self.unit = min(count, width)
        self.chunks = chunks
        self.rows = count // chunks
        self.keys = n_s * self.Sp
        group = max(1, 640 // self.keys)
        while self.rows % group:
            group -= 1
        self.group = group
        self.batches = None
        if group == self.rows and chunks == 5:
            self.batches = BATCHES
        self.staged = 1 if self.batches is None else max(len(b) for b in self.batches)

    def scratch(self, heads, width):
        return [
            pltpu.VMEM((self.P * self.S + self.Sp, width), F32),
            pltpu.VMEM((self.n_s, self.P * self.S, width), BF16),
            pltpu.VMEM((self.P // self.unit, heads, self.unit * self.Sp), F32),
            pltpu.VMEM((self.S // self.unit, self.n_s, heads, self.unit * self.Sp), F32),
            pltpu.VMEM((heads, self.Sp, self.keys), F32),
            pltpu.SemaphoreType.DMA((self.chunks, self.n_s)),
            pltpu.SemaphoreType.DMA((self.chunks, self.n_s)),
            pltpu.SemaphoreType.DMA((self.P // self.unit, self.n_p)),
            pltpu.SemaphoreType.DMA((self.S // self.unit, self.n_s)),
            pltpu.VMEM((self.n_s, self.staged * self.rows * self.S + self.Sp, width), F32),
            pltpu.VMEM((self.P * self.S + self.Sp, width), F32),
            pltpu.VMEM((8, self.keys), F32),
        ]

    def span(self, chunk):
        size = self.rows * self.S
        return pl.ds(aligned(chunk * size), size)

    def norm_rows(self, refs, chunk):
        x, buf = refs[:2]
        own = refs[10]
        rows = self.span(chunk)
        normed = layer_norm(x[rows])
        own[rows] = normed.astype(F32)
        buf[lax.axis_index(self.s_axis), rows] = normed

    def padded(self, tokens):
        row = lax.broadcasted_iota(jnp.int32, tokens.shape, 0)
        return jnp.where(row < self.S, tokens, 0.0).astype(BF16)

    def key_row(self, refs, values, fill):
        base = refs[11]
        base[...] = jnp.zeros_like(base)
        base[:, : self.n_s * self.S] = jnp.broadcast_to(values.astype(F32), (8, self.n_s * self.S))
        plain = base[...]
        lane = lax.broadcasted_iota(jnp.int32, plain.shape, 1)
        row = plain
        for b in range(1, self.n_s):
            turned = pltpu.roll(plain, (b * (self.Sp - self.S)) % self.keys, 1)
            row = jnp.where(lane // self.Sp == b, turned, row)
        return plain, jnp.where(lane % self.Sp < self.S, row, fill)

    def chain_row(self, refs, bias, weights, chain_ids):
        plain, row = self.key_row(refs, chain_ids, -2.0)
        shape = (self.Sp, self.keys)
        lane = lax.broadcasted_iota(jnp.int32, shape, 1)
        spot = lax.broadcasted_iota(jnp.int32, shape, 0) + lax.axis_index(self.s_axis) * self.S
        own = jnp.sum(jnp.where(lane == spot, plain[:1], 0.0), axis=-1, keepdims=True)
        same = jnp.where(own == row[:1], 1.0, 0.0)
        for h in range(bias.shape[0]):
            bias[h] = weights(h) * same

    def device(self, p_index, s_index):
        return {self.p_axis: p_index, self.s_axis: s_index}

    def send_rows(self, refs, chunk):
        x, buf, _, _, _, send, recv = refs[:7]
        mine = lax.axis_index(self.s_axis)
        rows = self.span(chunk)
        for step in range(1, self.n_s):
            peer = lax.rem(mine + step, self.n_s)
            pltpu.make_async_remote_copy(
                src_ref=buf.at[mine, rows],
                dst_ref=buf.at[mine, rows],
                send_sem=send.at[chunk, step],
                recv_sem=recv.at[chunk, mine],
                device_id=self.device(lax.axis_index(self.p_axis), peer),
                device_id_type=MESH,
            ).start()

    def wait_rows(self, refs, chunk):
        _, buf, _, _, _, _, recv = refs[:7]
        mine = lax.axis_index(self.s_axis)
        rows = self.span(chunk)
        for step in range(1, self.n_s):
            peer = lax.rem(mine + step, self.n_s)
            spot = buf.at[peer, rows]
            pltpu.make_async_copy(spot, spot, recv.at[chunk, peer]).wait()

    def piece(self, k):
        start = lax.axis_index(self.p_axis) * self.P + k * self.unit
        return start // self.S, lax.rem(start, self.S) // self.unit

    def bias_copies(self, refs, begin):
        _, _, part, got, _, _, _, send, recv = refs[:9]
        mine_p, mine_s = lax.axis_index(self.p_axis), lax.axis_index(self.s_axis)
        for k in range(self.P // self.unit):
            target, slot = self.piece(k)
            for step in range(self.n_p):
                row = lax.rem(mine_p + step, self.n_p)
                copy = pltpu.make_async_remote_copy(
                    src_ref=part.at[k],
                    dst_ref=got.at[slot, mine_s],
                    send_sem=send.at[k, step],
                    recv_sem=recv.at[slot, mine_s],
                    device_id=self.device(row, target),
                    device_id_type=MESH,
                )
                act = copy.start if begin else copy.wait_send
                if step > 0:
                    act()
                    continue
                pl.when(target != mine_s)(act)
                if begin:

                    @pl.when(target == mine_s)
                    def _():
                        pltpu.make_async_copy(
                            part.at[k], got.at[slot, mine_s], recv.at[slot, mine_s]
                        ).start()

    def send_bias(self, refs, weight):
        part, tokens = refs[2], refs[10]
        for k in range(self.P // self.unit):
            starts = [(k * self.unit + q) * self.S for q in range(self.unit)]
            own = [self.padded(tokens[at : at + self.Sp]) for at in starts]
            part[k] = dot_t(weight, jnp.concatenate(own, axis=0))
        self.bias_copies(refs, True)

    def finish_bias(self, refs):
        _, _, _, got, bias, _, _, _, recv = refs[:9]
        heads = bias.shape[0]
        share = max(1, LANES // self.Sp)
        for ks in range(self.S // self.unit):
            for b in range(self.n_s):
                spot = got.at[ks, b]
                pltpu.make_async_copy(spot, spot, recv.at[ks, b]).wait()
        lane = lax.broadcasted_iota(jnp.int32, (heads, LANES), 1) // min(self.Sp, LANES)
        for ks in range(self.S // self.unit):
            for q in range(self.unit):
                tile, off = (q * self.Sp) // LANES, (q * self.Sp) % LANES
                for first in range(0, self.n_s, share):
                    total = None
                    for b in range(first, min(first + share, self.n_s)):
                        turn = ((b - first) * self.Sp - off) % LANES
                        value = got[ks, b, :, tile * LANES : (tile + 1) * LANES]
                        if turn:
                            value = pltpu.roll(value, turn, 1)
                        total = value if total is None else jnp.where(lane == b - first, value, total)
                    where = first * self.Sp
                    width = min(LANES, self.keys - where)
                    spot = ks * self.unit + q
                    for h in range(heads):
                        bias[h, spot : spot + 1, where : where + width] += total[h : h + 1, :width]

    def wait_sends(self, refs):
        _, buf, _, _, _, send = refs[:6]
        mine = lax.axis_index(self.s_axis)
        for chunk in range(self.chunks):
            rows = self.span(chunk)
            spot = buf.at[mine, rows]
            for step in range(1, self.n_s):
                pltpu.make_async_copy(spot, spot, send.at[chunk, step]).wait()
        self.bias_copies(refs, False)

    def attend(self, refs, in_w, out_w, maskrow, consume):
        x, buf, _, _, bias = refs[:5]
        stage = refs[9]
        heads, width = bias.shape[0], x.shape[-1]
        head_width = width // heads
        scale = head_width ** (-0.5)
        mine = lax.axis_index(self.s_axis)
        Sp = self.Sp
        which = lax.broadcasted_iota(jnp.int32, (heads, 1, width), 2) // head_width
        select = which == lax.broadcasted_iota(jnp.int32, (heads, 1, width), 0)
        select_f = select.astype(F32)

        def step(chunk, index, group):
            local = index * (group * self.S)
            places = [local + r * self.S for r in range(group)]
            normed = [
                self.padded(stage[b, pl.ds(at, Sp)]) for at in places for b in range(self.n_s)
            ]
            normed = jnp.concatenate(normed, axis=0)
            own = jnp.concatenate([self.padded(stage[mine, pl.ds(at, Sp)]) for at in places], axis=0)
            keys = dot(normed, in_w[:, width : 2 * width]).astype(BF16)
            vals = dot(normed, in_w[:, 2 * width : 3 * width]).astype(BF16)
            keys = keys.reshape(group, self.keys, width)
            vals = vals.reshape(group, self.keys, width)
            ones = jnp.ones((self.keys, width), BF16)
            query = dot(own, in_w[:, :width]).astype(BF16).astype(F32).reshape(group, Sp, width)
            gate = dot(own, in_w[:, 3 * width :]).astype(BF16).astype(F32)
            table = bias[...].reshape(heads * Sp, self.keys)
            hidden = maskrow[:1]
            mixed = []
            for r in range(group):
                split = (query[r][None] * select_f).astype(BF16).reshape(heads * Sp, width)
                scores = dot_t(split, keys[r]) * scale
                scores = (scores + table) + hidden
                top = jnp.max(scores, axis=-1, keepdims=True)
                weights = jnp.exp(scores - top)
                both = dot(weights.astype(BF16), jnp.concatenate([vals[r], ones], axis=1))
                both = both.reshape(heads, Sp, 2 * width)
                total = jnp.sum(jnp.where(select, both[:, :, :width], 0.0), axis=0)
                norm = jnp.sum(jnp.where(select, both[:, :, width:], 0.0), axis=0)
                mixed.append(total / norm)
            mixed = mixed[0] if group == 1 else jnp.concatenate(mixed, axis=0)
            gated = (jax.nn.sigmoid(gate) * mixed).astype(BF16)
            begin = chunk * (self.rows * self.S)
            old = jnp.concatenate([x[pl.ds(begin + at, Sp)] for at in places], axis=0)
            consume(chunk * self.rows + index * group, (old + dot(gated, out_w[...])).astype(BF16).astype(F32))

        def fetch(chunk, place):
            self.wait_rows(refs, chunk)
            size = self.rows * self.S
            for b in range(self.n_s):
                stage[b, place * size : (place + 1) * size] = buf[b, self.span(chunk)].astype(F32)

        if self.batches is not None:
            for batch in self.batches:
                for place, chunk in enumerate(batch):
                    fetch(chunk, place)
                step(batch[0], 0, self.rows * len(batch))
            return

        @pl.loop(0, self.chunks)
        def _(chunk):
            fetch(chunk, 0)
            pl.loop(0, self.rows // self.group)(lambda index: step(chunk, index, self.group))


def send_all(phase, refs, weight):
    phase.norm_rows(refs, 0)
    phase.send_rows(refs, 0)
    for chunk in range(1, phase.chunks):
        phase.norm_rows(refs, chunk)
    phase.send_bias(refs, weight)
    for chunk in range(1, phase.chunks):
        phase.send_rows(refs, chunk)


def kernel(phases, sizes, pair, mask, chain_ids, chain_w, in_w, out_w, bias_w, up, down, result, *scratch):
    n_gr, n_gc = sizes
    one, two = phases
    refs1, refs2 = scratch[:12], scratch[12:24]
    middle, ending, mask1, mask2 = scratch[24:]
    x1, x2 = refs1[0], refs2[0]
    gr, gc = lax.axis_index("gr"), lax.axis_index("gc")
    barrier = pltpu.get_barrier_semaphore()
    for dr in range(n_gr):
        for dc in range(n_gc):
            if dr or dc:
                peer = {"gr": lax.rem(gr + dr, n_gr), "gc": lax.rem(gc + dc, n_gc)}
                pl.semaphore_signal(barrier, inc=1, device_id=peer, device_id_type=MESH)
    for phase, refs in ((one, refs1), (two, refs2)):
        for ref, used in ((refs[0], phase.P * phase.S), (refs[10], phase.P * phase.S)):
            ref[used:] = jnp.zeros((phase.Sp, ref.shape[-1]), F32)
        for b in range(phase.n_s):
            refs[9][b, phase.staged * phase.rows * phase.S :] = jnp.zeros((phase.Sp, x1.shape[-1]), F32)
    for row in range(one.P):
        x1[row * one.S : (row + 1) * one.S] = pair[row].astype(F32)
    maskadd = jnp.where(mask[...] > 0, 0.0, -1000000000.0).astype(F32)
    for a, phase, refs, hidden in ((0, one, refs1, mask1), (1, two, refs2, mask2)):
        phase.chain_row(refs, refs[4], lambda h, a=a: chain_w[a, h], chain_ids[...])
        hidden[...] = phase.key_row(refs, maskadd, PADDED)[1]
    pl.semaphore_wait(barrier, n_gr * n_gc - 1)
    send_all(one, refs1, bias_w[0])
    one.finish_bias(refs1)

    def transition(start, first):
        hidden = jnp.maximum(dot(layer_norm(first), up[...]), 0.0).astype(BF16)
        second = (first + dot(hidden, down[...])).astype(BF16).astype(F32)
        middle[pl.ds(aligned(start * one.Sp), second.shape[0]), :] = second

    one.attend(refs1, in_w.at[0], out_w.at[0], mask1, transition)
    for column in range(two.P):
        x2[column * two.S : (column + 1) * two.S] = middle[pl.ds(column, two.S, stride=one.Sp), :]
    send_all(two, refs2, bias_w[1])
    two.finish_bias(refs2)

    def keep(start, final):
        ending[pl.ds(aligned(start * two.Sp), final.shape[0]), :] = final

    two.attend(refs2, in_w.at[1], out_w.at[1], mask2, keep)
    for row in range(one.P):
        result[row] = ending[pl.ds(row, one.S, stride=two.Sp), :].astype(BF16)
    one.wait_sends(refs1)
    two.wait_sends(refs2)


def per_device(phases, sizes, pair, mask, chain_ids, attn_in, attn_out, bias_weight, chain_bias, trans_up, trans_down):
    one, two = phases
    width, heads = bias_weight.shape[1:]
    vmem = pl.BlockSpec(memory_space=pltpu.VMEM)
    smem = pl.BlockSpec(memory_space=pltpu.SMEM)
    return pl.pallas_call(
        functools.partial(kernel, phases, sizes),
        out_shape=jax.ShapeDtypeStruct(pair.shape, BF16),
        in_specs=[vmem] * 3 + [smem] + [vmem] * 5,
        out_specs=vmem,
        scratch_shapes=[
            *one.scratch(heads, width),
            *two.scratch(heads, width),
            pltpu.VMEM((one.P * one.Sp, width), F32),
            pltpu.VMEM((two.P * two.Sp, width), F32),
            pltpu.VMEM((8, one.keys), F32),
            pltpu.VMEM((8, two.keys), F32),
        ],
        compiler_params=pltpu.CompilerParams(
            collective_id=0, has_side_effects=True, vmem_limit_bytes=60 * 2**20
        ),
    )(
        pair,
        mask.reshape(1, -1),
        chain_ids.reshape(1, -1),
        chain_bias,
        attn_in,
        attn_out,
        jnp.transpose(bias_weight, (0, 2, 1)),
        trans_up,
        trans_down,
    )


def solution(mesh):
    sizes = (mesh.shape["gr"], mesh.shape["gc"])
    jobs = mesh.shape["jobs"]

    def whole(pair, *others):
        rows, columns = pair.shape[0] // (jobs * sizes[0]), pair.shape[1] // sizes[1]
        chunks = 5
        while rows % chunks or columns % chunks or (rows * columns // chunks) % 16:
            chunks -= 1
        phases = (
            Phase(rows, columns, sizes[0], sizes[1], "gr", "gc", chunks),
            Phase(columns, rows, sizes[1], sizes[0], "gc", "gr", chunks),
        )
        in_specs = (P(("jobs", "gr"), "gc", None), P("jobs"), P("jobs"), P(), P(), P(), P(), P(), P())
        return jax.shard_map(
            functools.partial(per_device, phases, sizes),
            mesh=mesh,
            in_specs=in_specs,
            out_specs=P(("jobs", "gr"), "gc", None),
            check_vma=False,
        )(pair, *others)

    return whole
```

```python
import functools

import jax
import jax.numpy as jnp
from jax import lax
from jax.experimental import pallas as pl
from jax.experimental.pallas import tpu as pltpu
from jax.sharding import PartitionSpec as P

F32 = jnp.float32
BF16 = jnp.bfloat16
MESH = pl.DeviceIdType.MESH
LANES = 128
PADDED = -3e38
BATCHES = {"gc": ((0,), (1, 2), (3, 4)), "gr": ((0, 1), (2, 3, 4))}


def padded_size(size):
    width = 16
    while width < size:
        width *= 2
    return width


def aligned(start):
    return start if isinstance(start, int) else pl.multiple_of(start, 16)


def layer_norm(floats):
    center = jnp.mean(floats, axis=-1, keepdims=True)
    moved = floats - center
    spread = jnp.mean(moved * moved, axis=-1, keepdims=True)
    return (moved * lax.rsqrt(spread + 1e-05)).astype(BF16)


def dot(left, right):
    return jnp.dot(left, right, preferred_element_type=F32)


def dot_t(left, right):
    return lax.dot_general(left, right, (((1,), (1,)), ((), ())), preferred_element_type=F32)


class Phase:
    def __init__(self, count, width, n_p, n_s, p_axis, s_axis, chunks):
        self.P, self.S, self.Sp = count, width, padded_size(width)
        self.n_p, self.n_s, self.p_axis, self.s_axis = n_p, n_s, p_axis, s_axis
        self.unit = min(count, width)
        self.chunks = chunks
        self.rows = count // chunks
        self.keys = n_s * self.Sp
        group = max(1, 640 // self.keys)
        while self.rows % group:
            group -= 1
        self.group = group
        self.batches = None
        if group == self.rows and chunks == 5:
            self.batches = BATCHES[s_axis]
        self.staged = 1 if self.batches is None else max(len(b) for b in self.batches)

    def scratch(self, heads, width):
        return [
            pltpu.VMEM((self.P * self.S + self.Sp, width), F32),
            pltpu.VMEM((self.n_s, self.P * self.S, width), BF16),
            pltpu.VMEM((self.P // self.unit, heads, self.unit * self.Sp), F32),
            pltpu.VMEM((self.S // self.unit, self.n_s, heads, self.unit * self.Sp), F32),
            pltpu.VMEM((heads, self.Sp, self.keys), F32),
            pltpu.SemaphoreType.DMA((self.chunks, self.n_s)),
            pltpu.SemaphoreType.DMA((self.chunks, self.n_s)),
            pltpu.SemaphoreType.DMA((self.P // self.unit, self.n_p)),
            pltpu.SemaphoreType.DMA((self.S // self.unit, self.n_s)),
            pltpu.VMEM((self.n_s, self.staged * self.rows * self.S + self.Sp, width), F32),
            pltpu.VMEM((self.P * self.S + self.Sp, width), F32),
            pltpu.VMEM((8, self.keys), F32),
        ]

    def span(self, chunk):
        size = self.rows * self.S
        return pl.ds(aligned(chunk * size), size)

    def norm_rows(self, refs, chunk):
        x, buf = refs[:2]
        own = refs[10]
        rows = self.span(chunk)
        normed = layer_norm(x[rows])
        own[rows] = normed.astype(F32)
        buf[lax.axis_index(self.s_axis), rows] = normed

    def padded(self, tokens):
        row = lax.broadcasted_iota(jnp.int32, tokens.shape, 0)
        return jnp.where(row < self.S, tokens, 0.0).astype(BF16)

    def key_row(self, refs, values, fill):
        base = refs[11]
        base[...] = jnp.zeros_like(base)
        base[:, : self.n_s * self.S] = jnp.broadcast_to(values.astype(F32), (8, self.n_s * self.S))
        plain = base[...]
        lane = lax.broadcasted_iota(jnp.int32, plain.shape, 1)
        row = plain
        for b in range(1, self.n_s):
            turned = pltpu.roll(plain, (b * (self.Sp - self.S)) % self.keys, 1)
            row = jnp.where(lane // self.Sp == b, turned, row)
        return plain, jnp.where(lane % self.Sp < self.S, row, fill)

    def chain_row(self, refs, bias, weights, chain_ids):
        plain, row = self.key_row(refs, chain_ids, -2.0)
        shape = (self.Sp, self.keys)
        lane = lax.broadcasted_iota(jnp.int32, shape, 1)
        spot = lax.broadcasted_iota(jnp.int32, shape, 0) + lax.axis_index(self.s_axis) * self.S
        own = jnp.sum(jnp.where(lane == spot, plain[:1], 0.0), axis=-1, keepdims=True)
        same = jnp.where(own == row[:1], 1.0, 0.0)
        for h in range(bias.shape[0]):
            bias[h] = weights(h) * same

    def device(self, p_index, s_index):
        return {self.p_axis: p_index, self.s_axis: s_index}

    def send_rows(self, refs, chunk):
        x, buf, _, _, _, send, recv = refs[:7]
        mine = lax.axis_index(self.s_axis)
        rows = self.span(chunk)
        for step in sorted(range(1, self.n_s), key=lambda step: -min(step, self.n_s - step)):
            peer = lax.rem(mine + step, self.n_s)
            pltpu.make_async_remote_copy(
                src_ref=buf.at[mine, rows],
                dst_ref=buf.at[mine, rows],
                send_sem=send.at[chunk, step],
                recv_sem=recv.at[chunk, mine],
                device_id=self.device(lax.axis_index(self.p_axis), peer),
                device_id_type=MESH,
            ).start()

    def wait_rows(self, refs, chunk):
        _, buf, _, _, _, _, recv = refs[:7]
        mine = lax.axis_index(self.s_axis)
        rows = self.span(chunk)
        for step in range(1, self.n_s):
            peer = lax.rem(mine + step, self.n_s)
            spot = buf.at[peer, rows]
            pltpu.make_async_copy(spot, spot, recv.at[chunk, peer]).wait()

    def piece(self, k):
        start = lax.axis_index(self.p_axis) * self.P + k * self.unit
        return start // self.S, lax.rem(start, self.S) // self.unit

    def bias_copies(self, refs, begin):
        _, _, part, got, _, _, _, send, recv = refs[:9]
        mine_p, mine_s = lax.axis_index(self.p_axis), lax.axis_index(self.s_axis)
        for k in range(self.P // self.unit):
            target, slot = self.piece(k)
            for step in range(self.n_p):
                row = lax.rem(mine_p + step, self.n_p)
                copy = pltpu.make_async_remote_copy(
                    src_ref=part.at[k],
                    dst_ref=got.at[slot, mine_s],
                    send_sem=send.at[k, step],
                    recv_sem=recv.at[slot, mine_s],
                    device_id=self.device(row, target),
                    device_id_type=MESH,
                )
                act = copy.start if begin else copy.wait_send
                if step > 0:
                    act()
                    continue
                pl.when(target != mine_s)(act)
                if begin:

                    @pl.when(target == mine_s)
                    def _():
                        pltpu.make_async_copy(
                            part.at[k], got.at[slot, mine_s], recv.at[slot, mine_s]
                        ).start()

    def send_bias(self, refs, weight):
        part, tokens = refs[2], refs[10]
        for k in range(self.P // self.unit):
            starts = [(k * self.unit + q) * self.S for q in range(self.unit)]
            own = [self.padded(tokens[at : at + self.Sp]) for at in starts]
            part[k] = dot_t(weight, jnp.concatenate(own, axis=0))
        self.bias_copies(refs, True)

    def finish_bias(self, refs):
        _, _, _, got, bias, _, _, _, recv = refs[:9]
        heads = bias.shape[0]
        share = max(1, LANES // self.Sp)
        for ks in range(self.S // self.unit):
            for b in range(self.n_s):
                spot = got.at[ks, b]
                pltpu.make_async_copy(spot, spot, recv.at[ks, b]).wait()
        lane = lax.broadcasted_iota(jnp.int32, (heads, LANES), 1) // min(self.Sp, LANES)
        for ks in range(self.S // self.unit):
            for q in range(self.unit):
                tile, off = (q * self.Sp) // LANES, (q * self.Sp) % LANES
                for first in range(0, self.n_s, share):
                    total = None
                    for b in range(first, min(first + share, self.n_s)):
                        turn = ((b - first) * self.Sp - off) % LANES
                        value = got[ks, b, :, tile * LANES : (tile + 1) * LANES]
                        if turn:
                            value = pltpu.roll(value, turn, 1)
                        total = value if total is None else jnp.where(lane == b - first, value, total)
                    where = first * self.Sp
                    width = min(LANES, self.keys - where)
                    spot = ks * self.unit + q
                    for h in range(heads):
                        bias[h, spot : spot + 1, where : where + width] += total[h : h + 1, :width]

    def wait_sends(self, refs):
        _, buf, _, _, _, send = refs[:6]
        mine = lax.axis_index(self.s_axis)
        for chunk in range(self.chunks):
            rows = self.span(chunk)
            spot = buf.at[mine, rows]
            for step in range(1, self.n_s):
                pltpu.make_async_copy(spot, spot, send.at[chunk, step]).wait()
        self.bias_copies(refs, False)

    def attend(self, refs, in_w, out_w, maskrow, consume):
        x, buf, _, _, bias = refs[:5]
        stage = refs[9]
        heads, width = bias.shape[0], x.shape[-1]
        head_width = width // heads
        scale = head_width ** (-0.5)
        mine = lax.axis_index(self.s_axis)
        Sp = self.Sp
        which = lax.broadcasted_iota(jnp.int32, (heads, 1, width), 2) // head_width
        select = which == lax.broadcasted_iota(jnp.int32, (heads, 1, width), 0)
        select_f = select.astype(F32)

        def step(chunk, index, group):
            local = index * (group * self.S)
            places = [local + r * self.S for r in range(group)]
            normed = [
                self.padded(stage[b, pl.ds(at, Sp)]) for at in places for b in range(self.n_s)
            ]
            normed = jnp.concatenate(normed, axis=0)
            own = jnp.concatenate([self.padded(stage[mine, pl.ds(at, Sp)]) for at in places], axis=0)
            keys = dot(normed, in_w[:, width : 2 * width]).astype(BF16)
            vals = dot(normed, in_w[:, 2 * width : 3 * width]).astype(BF16)
            keys = keys.reshape(group, self.keys, width)
            vals = vals.reshape(group, self.keys, width)
            ones = jnp.ones((self.keys, width), BF16)
            query = dot(own, in_w[:, :width]).astype(BF16).astype(F32).reshape(group, Sp, width)
            gate = dot(own, in_w[:, 3 * width :]).astype(BF16).astype(F32)
            table = bias[...].reshape(heads * Sp, self.keys)
            hidden = maskrow[:1]
            mixed = []
            for r in range(group):
                split = (query[r][None] * select_f).astype(BF16).reshape(heads * Sp, width)
                scores = dot_t(split, keys[r]) * scale
                scores = (scores + table) + hidden
                top = jnp.max(scores, axis=-1, keepdims=True)
                weights = jnp.exp(scores - top)
                both = dot(weights.astype(BF16), jnp.concatenate([vals[r], ones], axis=1))
                both = both.reshape(heads, Sp, 2 * width)
                total = jnp.sum(jnp.where(select, both[:, :, :width], 0.0), axis=0)
                norm = jnp.sum(jnp.where(select, both[:, :, width:], 0.0), axis=0)
                mixed.append(total / norm)
            mixed = mixed[0] if group == 1 else jnp.concatenate(mixed, axis=0)
            gated = (jax.nn.sigmoid(gate) * mixed).astype(BF16)
            begin = chunk * (self.rows * self.S)
            old = jnp.concatenate([x[pl.ds(begin + at, Sp)] for at in places], axis=0)
            consume(chunk * self.rows + index * group, (old + dot(gated, out_w[...])).astype(BF16).astype(F32))

        def fetch(chunk, place):
            self.wait_rows(refs, chunk)
            size = self.rows * self.S
            for b in range(self.n_s):
                stage[b, place * size : (place + 1) * size] = buf[b, self.span(chunk)].astype(F32)

        if self.batches is not None:
            for batch in self.batches:
                for place, chunk in enumerate(batch):
                    fetch(chunk, place)
                step(batch[0], 0, self.rows * len(batch))
            return

        @pl.loop(0, self.chunks)
        def _(chunk):
            fetch(chunk, 0)
            pl.loop(0, self.rows // self.group)(lambda index: step(chunk, index, self.group))


def send_all(phase, refs, weight):
    for chunk in range(phase.chunks):
        phase.norm_rows(refs, chunk)
    phase.send_bias(refs, weight)
    for chunk in range(phase.chunks):
        phase.send_rows(refs, chunk)


def kernel(phases, sizes, pair, mask, chain_ids, chain_w, in_w, out_w, bias_w, up, down, result, *scratch):
    n_gr, n_gc = sizes
    one, two = phases
    refs1, refs2 = scratch[:12], scratch[12:24]
    middle, ending, mask1, mask2 = scratch[24:]
    x1, x2 = refs1[0], refs2[0]
    gr, gc = lax.axis_index("gr"), lax.axis_index("gc")
    barrier = pltpu.get_barrier_semaphore()
    for dr in range(n_gr):
        for dc in range(n_gc):
            if dr or dc:
                peer = {"gr": lax.rem(gr + dr, n_gr), "gc": lax.rem(gc + dc, n_gc)}
                pl.semaphore_signal(barrier, inc=1, device_id=peer, device_id_type=MESH)
    for phase, refs in ((one, refs1), (two, refs2)):
        for ref, used in ((refs[0], phase.P * phase.S), (refs[10], phase.P * phase.S)):
            ref[used:] = jnp.zeros((phase.Sp, ref.shape[-1]), F32)
        for b in range(phase.n_s):
            refs[9][b, phase.staged * phase.rows * phase.S :] = jnp.zeros((phase.Sp, x1.shape[-1]), F32)
    for row in range(one.P):
        x1[row * one.S : (row + 1) * one.S] = pair[row].astype(F32)
    maskadd = jnp.where(mask[...] > 0, 0.0, -1000000000.0).astype(F32)
    for a, phase, refs, hidden in ((0, one, refs1, mask1), (1, two, refs2, mask2)):
        phase.chain_row(refs, refs[4], lambda h, a=a: chain_w[a, h], chain_ids[...])
        hidden[...] = phase.key_row(refs, maskadd, PADDED)[1]
    pl.semaphore_wait(barrier, n_gr * n_gc - 1)
    send_all(one, refs1, bias_w[0])
    one.finish_bias(refs1)

    def transition(start, first):
        hidden = jnp.maximum(dot(layer_norm(first), up[...]), 0.0).astype(BF16)
        second = (first + dot(hidden, down[...])).astype(BF16).astype(F32)
        middle[pl.ds(aligned(start * one.Sp), second.shape[0]), :] = second

    one.attend(refs1, in_w.at[0], out_w.at[0], mask1, transition)
    for column in range(two.P):
        x2[column * two.S : (column + 1) * two.S] = middle[pl.ds(column, two.S, stride=one.Sp), :]
    send_all(two, refs2, bias_w[1])
    two.finish_bias(refs2)

    def keep(start, final):
        ending[pl.ds(aligned(start * two.Sp), final.shape[0]), :] = final

    two.attend(refs2, in_w.at[1], out_w.at[1], mask2, keep)
    for row in range(one.P):
        result[row] = ending[pl.ds(row, one.S, stride=two.Sp), :].astype(BF16)
    one.wait_sends(refs1)
    two.wait_sends(refs2)


def per_device(phases, sizes, pair, mask, chain_ids, attn_in, attn_out, bias_weight, chain_bias, trans_up, trans_down):
    one, two = phases
    width, heads = bias_weight.shape[1:]
    vmem = pl.BlockSpec(memory_space=pltpu.VMEM)
    smem = pl.BlockSpec(memory_space=pltpu.SMEM)
    return pl.pallas_call(
        functools.partial(kernel, phases, sizes),
        out_shape=jax.ShapeDtypeStruct(pair.shape, BF16),
        in_specs=[vmem] * 3 + [smem] + [vmem] * 5,
        out_specs=vmem,
        scratch_shapes=[
            *one.scratch(heads, width),
            *two.scratch(heads, width),
            pltpu.VMEM((one.P * one.Sp, width), F32),
            pltpu.VMEM((two.P * two.Sp, width), F32),
            pltpu.VMEM((8, one.keys), F32),
            pltpu.VMEM((8, two.keys), F32),
        ],
        compiler_params=pltpu.CompilerParams(
            collective_id=0, has_side_effects=True, vmem_limit_bytes=60 * 2**20
        ),
    )(
        pair,
        mask.reshape(1, -1),
        chain_ids.reshape(1, -1),
        chain_bias,
        attn_in,
        attn_out,
        jnp.transpose(bias_weight, (0, 2, 1)),
        trans_up,
        trans_down,
    )


def solution(mesh):
    sizes = (mesh.shape["gr"], mesh.shape["gc"])
    jobs = mesh.shape["jobs"]

    def whole(pair, *others):
        rows, columns = pair.shape[0] // (jobs * sizes[0]), pair.shape[1] // sizes[1]
        chunks = 5
        while rows % chunks or columns % chunks or (rows * columns // chunks) % 16:
            chunks -= 1
        phases = (
            Phase(rows, columns, sizes[0], sizes[1], "gr", "gc", chunks),
            Phase(columns, rows, sizes[1], sizes[0], "gc", "gr", chunks),
        )
        in_specs = (P(("jobs", "gr"), "gc", None), P("jobs"), P("jobs"), P(), P(), P(), P(), P(), P())
        return jax.shard_map(
            functools.partial(per_device, phases, sizes),
            mesh=mesh,
            in_specs=in_specs,
            out_specs=P(("jobs", "gr"), "gc", None),
            check_vma=False,
        )(pair, *others)

    return whole
```
